256 devices in a mesh: kvh: 8 (over x, core), store: 32 (over y, z).
Axes of the slice: x: 4, y: 4, z: 8, core: 2. Of those that a mesh axis runs over, the one named last changes fastest.
Arguments:
- query_heads: bfloat16 [1024, 8, 8, 128], P('store', 'kvh'), may hold values from -1024 to 1024
- span_keys: bfloat16 [512, 8, 512, 128], P('store', 'kvh'), may hold values from -4 to 4
- span_values: bfloat16 [512, 8, 512, 128], P('store', 'kvh'), may hold values from -6 to 6
- cited_spans: int32 [1024, 32], P('store'), may hold values from 0 to 511, as said below
- cite_count: int32 [1024], P('store'), may hold values from 8 to 32, as said below
- out_weight: bfloat16 [8192, 8192], P('kvh', 'store'), may hold values from -0.0625 to 0.0625
Outputs:
- mixed: bfloat16 [1024, 8192], P('kvh', 'store')
The draws below stay inside these ranges and needn't reach their ends.
Inputs may be any that keep to these rules, and one draw needn't show every extreme that they name: `cited_spans`: the first cite_count[r] entries of a row are distinct span ids; the later entries are ids of spans cited by rows of the same store index and are not read. Among the entries that are read, the rows of one store index cite exactly 2 distinct spans of each store shard (span c is held by store index c // 16). `cite_count`: the first row of each store index cites 32 spans.
All inputs are finite; a program needn't handle non-finite values.
Results may differ from the reference program's by a relative error of at most 0.005.
Values may be sent and summed in bfloat16 or wider, within the bound.
No kernel may reach another device: no remote copies, remote signals or barrier semaphores. Data moves between devices by JAX's collectives and lax.ppermute only.
A program may use at most 128 MiB of HBM per device.

```python
import jax
import jax.numpy as jnp
from jax import lax

D = 8192
KVH = 8
G = 8
HD = 128
CT = 512
MINC = 8
MAXC = 32
POOL = 64
CH_DEV = 16
ROWS_DEV = 32
PER_OWNER = 2
NCHUNK = 512
ROWS = 1024


def cite_table(key):
    key = jax.random.fold_in(key, 11)
    groups = ROWS // ROWS_DEV
    owners = NCHUNK // CH_DEV
    key_fame, key_noise, key_count, key_order = jax.random.split(key, 4)
    fame = jax.random.randint(key_fame, (owners, CH_DEV), 0, 4)
    noise = jax.random.randint(key_noise, (groups, owners, CH_DEV), 0, 4096)
    order_score = (fame[None] * 4096 + noise) * CH_DEV + jnp.arange(CH_DEV, dtype=jnp.int32)
    picked = jnp.argsort(order_score, axis=-1)[..., :PER_OWNER].astype(jnp.int32)
    shard_start = jnp.arange(owners, dtype=jnp.int32) * CH_DEV
    pool_ids = (picked + shard_start[None, :, None]).reshape(groups, POOL)
    row_index = jnp.arange(ROWS, dtype=jnp.int32)
    counts = jax.random.randint(key_count, (ROWS,), MINC, MAXC + 1)
    counts = jnp.where(row_index % ROWS_DEV == 0, MAXC, counts)
    cover = (POOL + ROWS_DEV - 1) // ROWS_DEV
    place = jnp.arange(POOL, dtype=jnp.int32)
    row_local = row_index % ROWS_DEV
    priority = jax.random.randint(key_order, (ROWS, POOL), 0, 4096) * POOL + place[None, :]
    assigned = place[None, :] // cover == row_local[:, None]
    priority = jnp.where(assigned, priority - 4096 * POOL, priority)
    chosen = jnp.argsort(priority, axis=-1)[:, :MAXC].astype(jnp.int32)
    row_group = row_index // ROWS_DEV
    span_ids = jnp.take_along_axis(pool_ids[row_group], chosen, axis=-1)
    return (span_ids.astype(jnp.int32), counts.astype(jnp.int32))


def span_key_draw(key, span_list):
    base = jax.random.fold_in(key, 23)

    def single_span(span_id):
        normal_keys = jax.random.normal(jax.random.fold_in(base, span_id), (KVH, CT, HD), jnp.float32)
        return jnp.clip(normal_keys, -4.0, 4.0)
    return jax.vmap(single_span)(span_list)


def draw_cited_spans(key, part):
    return cite_table(key)[0]


def draw_cite_count(key, part):
    return cite_table(key)[1]


def draw_span_keys(key, part):
    return span_key_draw(key, jnp.arange(NCHUNK, dtype=jnp.int32)).astype(jnp.bfloat16)


def draw_span_values(key, part):
    key = jax.random.fold_in(key, 41)
    key_mean, key_token = jax.random.split(key)
    span_mean = jax.random.normal(key_mean, (NCHUNK, KVH, 1, HD), jnp.float32)
    token_part = 0.7 * jax.random.normal(key_token, (NCHUNK, KVH, CT, HD), jnp.float32)
    return jnp.clip(span_mean + token_part, -6.0, 6.0).astype(jnp.bfloat16)


def draw_query_heads(key, part):
    key = jax.random.fold_in(key, 37)
    key_base = jax.random.fold_in(key, 0)
    queries = jnp.clip(1.3 * jax.random.normal(key_base, (ROWS, KVH, G, HD), jnp.float32), -5.0, 5.0)
    return queries.astype(jnp.bfloat16)


def levels(key, dims, cuts, smallest, high):
    gain = 1.0
    for position, blocks in cuts:
        steps = jax.random.uniform(jax.random.fold_in(jax.random.fold_in(key, 6), position), (blocks,), jnp.float32, smallest / len(cuts), high / len(cuts))
        gain = gain * jnp.repeat(jnp.exp(steps), dims[position] // blocks).reshape((-1,) + (1,) * (len(dims) - 1 - position))
    return gain


def centred(rng, extent, scale, reach, shards=(), held_as=jnp.bfloat16):
    gain = levels(rng, extent, shards, -0.22, 0.18) if shards else 1.0
    values = jax.random.normal(rng, extent, jnp.float32) * scale * gain
    return jnp.minimum(jnp.maximum(values, -reach), reach).astype(held_as)


def setup_inputs(seed: int = 0) -> dict:
    splits = jax.random.split(jax.random.key(seed), 7)
    query_heads = draw_query_heads(jax.random.fold_in(splits[6], 71), 0)
    span_keys = draw_span_keys(jax.random.fold_in(splits[6], 71), 0)
    span_values = draw_span_values(jax.random.fold_in(splits[6], 71), 0)
    cited_spans = draw_cited_spans(jax.random.fold_in(splits[6], 71), 0)
    cite_count = draw_cite_count(jax.random.fold_in(splits[6], 71), 0)
    out_weight = centred(splits[5], (KVH * G * HD, D), (KVH * G * HD) ** -0.5, 0.0625, ((0, 8), (1, 32)))
    return {"query_heads": query_heads, "span_keys": span_keys, "span_values": span_values, "cited_spans": cited_spans, "cite_count": cite_count, "out_weight": out_weight}


def reference(query_heads, span_keys, span_values, cited_spans, cite_count, out_weight):
    score_scale = HD ** -0.5
    slot_index = jnp.arange(MAXC, dtype=jnp.int32)

    def attend_row(inputs):
        query_row, row_ids, row_total = inputs
        row_keys = span_keys[row_ids].astype(jnp.float32)
        row_values = span_values[row_ids].astype(jnp.float32)
        scores = jnp.einsum("kgd,jktd->kgjt", query_row.astype(jnp.float32), row_keys) * score_scale
        span_top = jnp.max(scores, axis=-1)
        probs = jnp.exp(scores - span_top[..., None])
        rounded = lax.optimization_barrier(probs.astype(jnp.bfloat16)).astype(jnp.float32)
        span_sum = jnp.sum(probs, axis=-1)
        span_out = jnp.einsum("kgjt,jktd->kgjd", rounded, row_values)
        slot_live = slot_index < row_total
        row_top = jnp.max(jnp.where(slot_live, span_top, -1e30), axis=-1)
        weights = jnp.where(slot_live, jnp.exp(span_top - row_top[..., None]), 0.0)
        numer = jnp.sum(weights[..., None] * span_out, axis=2)
        denom = jnp.sum(weights * span_sum, axis=-1)
        return (numer / denom[..., None]).astype(jnp.bfloat16)

    attn = lax.map(attend_row, (query_heads, cited_spans, cite_count))
    flat_attn = attn.reshape(ROWS, KVH * G * HD)
    return jnp.dot(flat_attn, out_weight, preferred_element_type=jnp.float32).astype(jnp.bfloat16)
```

```python
import functools
import math

import jax
import jax.numpy as jnp
from jax import lax
from jax.experimental import pallas as pl
from jax.experimental.pallas import tpu as pltpu
from jax.sharding import Mesh, PartitionSpec as P

HEADS = 8
HEAD = 128
FLAT = HEADS * HEAD
WIDE = FLAT + 128
NEG = -1e30
BIG = 1e30
EXP_SCALE = HEAD**-0.5 * math.log2(math.e)
F32 = jnp.float32
BF16 = jnp.bfloat16
VMEM_LIMIT = 48 * 1024 * 1024


def shift(x, axis, size, step):
    return lax.ppermute(x, axis, [(i, (i + step) % size) for i in range(size)])


def lane_ids(rows):
    return lax.broadcasted_iota(jnp.int32, (rows, 128), 1)


def pack_stats(top_then_sum, rows):
    lane = lane_ids(rows)
    high = top_then_sum.astype(BF16).astype(F32)
    rest = top_then_sum - high
    middle = rest.astype(BF16).astype(F32)
    low = rest - middle
    place = (lane // 8) % 3
    terms = jnp.where(place == 0, high, jnp.where(place == 1, middle, low))
    return jnp.where(lane < 48, terms, 0.0).astype(BF16)


def unpack_stats(packed):
    terms = packed.astype(F32)
    return terms + (pltpu.roll(terms, 120, 1) + pltpu.roll(terms, 112, 1))


def attend_group(me, q, k_ref, v_ref):
    rows = q.shape[0]
    code = q[:, FLAT:].astype(F32)
    span = jnp.where(code > 0, code - 1.0, 255.0 - code) - 16.0 * me
    mine = (code != 0) & (span >= 0) & (span < 16)
    first = jnp.min(jnp.where(mine, span, 99.0))
    second = jnp.max(jnp.where(mine, span, -1.0))
    picks = []
    for chosen in (first, second):
        live = jnp.max(jnp.where(mine & (span == chosen), 1.0, 0.0), axis=1, keepdims=True)
        at = jnp.clip(chosen.astype(jnp.int32), 0, 15)
        picks.append((at, jnp.concatenate([live] * HEADS, axis=0) > 0))
    queries = jnp.concatenate([q[:, h * HEAD : (h + 1) * HEAD] for h in range(HEADS)], axis=0)
    scores = [
        lax.dot_general(
            queries, k_ref[at], (((1,), (1,)), ((), ())), preferred_element_type=F32
        )
        for at, _ in picks
    ]
    top = None
    for s, (_, live) in zip(scores, picks):
        span_top = jnp.where(live, jnp.max(s, axis=1, keepdims=True), NEG)
        top = span_top if top is None else jnp.maximum(top, span_top)
    numer, denom = None, None
    for s, (at, live) in zip(scores, picks):
        probs = jnp.exp2((s - jnp.where(live, top, BIG)) * EXP_SCALE)
        total = jnp.sum(probs, axis=1, keepdims=True)
        out = jnp.dot(probs.astype(BF16), v_ref[at], preferred_element_type=F32)
        numer = out if numer is None else numer + out
        denom = total if denom is None else denom + total
    lane = lane_ids(rows)
    stats = jnp.zeros((rows, 128), F32)
    for h in range(HEADS):
        part = slice(h * rows, (h + 1) * rows)
        stats = jnp.where(
            lane % 8 == h, jnp.where(lane < 24, top[part], denom[part]), stats
        )
    heads = [numer[h * rows : (h + 1) * rows].astype(BF16) for h in range(HEADS)]
    return jnp.concatenate(heads + [pack_stats(stats, rows)], axis=1)


def attend_kernel(blocks, me_ref, *refs):
    q_refs, (k_ref, v_ref), out_refs = refs[:blocks], refs[blocks : blocks + 2], refs[blocks + 2 :]
    me = me_ref[0].astype(F32)
    for q_ref, out_ref in zip(q_refs, out_refs):

        @pl.loop(0, q_ref.shape[0])
        def _(g):
            out_ref[g] = attend_group(me, q_ref[g], k_ref, v_ref)


def attend(me, blocks, keys, values):
    vmem = pl.BlockSpec(memory_space=pltpu.VMEM)
    groups = sum(b.shape[0] for b in blocks)
    return pl.pallas_call(
        functools.partial(attend_kernel, len(blocks)),
        out_shape=[jax.ShapeDtypeStruct(b.shape, BF16) for b in blocks],
        in_specs=[pl.BlockSpec(memory_space=pltpu.SMEM)] + [vmem] * (len(blocks) + 2),
        out_specs=[vmem] * len(blocks),
        compiler_params=pltpu.CompilerParams(vmem_limit_bytes=VMEM_LIMIT),
        cost_estimate=pl.CostEstimate(
            flops=groups * 4 * 256 * 1024 * 128,
            bytes_accessed=keys.size * 4 + groups * 32 * WIDE * 4,
            transcendentals=groups * 256 * 1024,
        ),
        name="attend",
    )(me, *blocks, keys, values)


def merge_rows(parts, final):
    rows = parts[0].shape[0]
    stats = [unpack_stats(p[:, FLAT:]) for p in parts]
    top = functools.reduce(jnp.maximum, stats)
    weights = [jnp.exp2((s - top) * EXP_SCALE) for s in stats]
    denom = functools.reduce(
        jnp.add, [pltpu.roll(w, 24, 1) * s for w, s in zip(weights, stats)]
    )
    heads = []
    for h in range(HEADS):
        lanes = slice(h * HEAD, (h + 1) * HEAD)
        numer = functools.reduce(
            jnp.add, [w[:, h : h + 1] * p[:, lanes].astype(F32) for w, p in zip(weights, parts)]
        )
        heads.append((numer / denom[:, 24 + h : 25 + h] if final else numer).astype(BF16))
    if final:
        return jnp.concatenate(heads, axis=1)
    lane = lane_ids(rows)
    tops = jnp.where(lane < 8, top, jnp.where(lane < 16, pltpu.roll(top, 8, 1), pltpu.roll(top, 16, 1)))
    sums = jnp.where(
        lane < 32, denom, jnp.where(lane < 40, pltpu.roll(denom, 8, 1), pltpu.roll(denom, 16, 1))
    )
    return jnp.concatenate(heads + [pack_stats(jnp.where(lane < 24, tops, sums), rows)], axis=1)


def merge_kernel(plan, n_in, final, *refs):
    ins, outs = refs[:n_in], refs[n_in:]
    for out_ref, entries in zip(outs, plan):
        for g, sources in enumerate(entries):
            parts = [ins[i][j] for i, j in sources]
            if len(parts) == 1 and not final:
                out_ref[g] = parts[0]
            elif len(out_ref.shape) == 3:
                out_ref[g] = merge_rows(parts, final)
            else:
                out_ref[...] = merge_rows(parts, final)


def merge(inputs, plan, final=False):
    vmem = pl.BlockSpec(memory_space=pltpu.VMEM)
    if final:
        out_shape = [jax.ShapeDtypeStruct((inputs[0].shape[1], FLAT), BF16)]
    else:
        out_shape = [
            jax.ShapeDtypeStruct((len(entries),) + inputs[0].shape[1:], BF16) for entries in plan
        ]
    size = sum(i.size for i in inputs)
    return pl.pallas_call(
        functools.partial(merge_kernel, plan, len(inputs), final),
        out_shape=out_shape,
        in_specs=[vmem] * len(inputs),
        out_specs=[vmem] * len(out_shape),
        compiler_params=pltpu.CompilerParams(vmem_limit_bytes=VMEM_LIMIT),
        cost_estimate=pl.CostEstimate(flops=4 * size, bytes_accessed=4 * size, transcendentals=0),
        name="merge",
    )(*inputs)


def project_kernel(here_ref, *refs):
    block_refs, w_ref, (keep_ref, give_ref) = refs[:8], refs[8], refs[9:]
    x, core, y, z = here_ref[0], here_ref[1], here_ref[2], here_ref[3]
    for step, ref in zip((0, -1, 1, -2, 2, -3, 3, 4), block_refs):
        source = lax.rem(z + step + 8, 8)
        out = jnp.dot(
            ref[...].reshape(128, FLAT), w_ref[...], preferred_element_type=F32
        )
        stays = source // 4 == core
        for back in range(4):
            ahead = lax.rem(y - back - x + 8, 4)
            rows = out[back * 32 : back * 32 + 32]

            @pl.when(stays)
            def _():
                keep_ref[ahead, source % 4] = rows

            @pl.when(jnp.logical_not(stays))
            def _():
                give_ref[ahead, source % 4] = rows


def project(here, blocks, weight):
    vmem = pl.BlockSpec(memory_space=pltpu.VMEM)
    out = jax.ShapeDtypeStruct((4, 4, 32, weight.shape[1]), F32)
    return pl.pallas_call(
        project_kernel,
        out_shape=[out, out],
        in_specs=[pl.BlockSpec(memory_space=pltpu.SMEM)] + [vmem] * 9,
        out_specs=[vmem, vmem],
        compiler_params=pltpu.CompilerParams(vmem_limit_bytes=VMEM_LIMIT),
        cost_estimate=pl.CostEstimate(
            flops=2 * 1024 * 1024 * 256, bytes_accessed=4 * 2**20, transcendentals=0
        ),
        name="project",
    )(here, *blocks, weight)


def gather_y(x):
    return jnp.stack([x] + [shift(x, "y", 4, step) for step in (1, 2, 3)])


def gather_z(block):
    blocks, low, high = [block], block, block
    for _ in range(3):
        low, high = shift(low, "z", 8, 1), shift(high, "z", 8, -1)
        blocks += [low, high]
    far = jnp.concatenate([shift(low[:2], "z", 8, 1), shift(high[2:], "z", 8, -1)])
    return blocks + [far]


def per_device(query_heads, span_keys, span_values, cited_spans, cite_count, out_weight):
    rows = query_heads.shape[0]
    y, z = lax.axis_index("y"), lax.axis_index("z")
    here = jnp.stack([lax.axis_index("x"), lax.axis_index("core"), y, z]).astype(jnp.int32)
    me = (y * 8 + z).astype(jnp.int32).reshape(1)
    slot = jnp.arange(cited_spans.shape[1], dtype=jnp.int32)
    code = jnp.where(cited_spans < 256, cited_spans + 1, 255 - cited_spans)
    code = jnp.where(slot[None, :] < cite_count[:, None], code, 0).astype(BF16)
    wide = jnp.concatenate(
        [query_heads.reshape(rows, FLAT), code, jnp.zeros((rows, 128 - code.shape[1]), BF16)], axis=1
    )
    keys, values = span_keys[:, 0], span_values[:, 0]

    blocks = gather_z(gather_y(wide))
    own, b1, a1, b2, a2, b3, a3, far = blocks
    (p_own,) = attend(me, [own], keys, values)
    p_b1, p_a1 = attend(me, [b1, a1], keys, values)
    p_b2, p_a2 = attend(me, [b2, a2], keys, values)
    p_b3, p_a3 = attend(me, [b3, a3], keys, values)
    (p_far,) = attend(me, [far], keys, values)

    both = lambda i, j: [[(i, g), (j, g)] for g in range(4)]
    down, up = shift(p_far[:2], "z", 8, -1), shift(p_far[2:], "z", 8, 1)
    to_b, to_a = merge(
        [p_b3, p_a3, down, up],
        [
            [[(0, 0), (2, 0)], [(0, 1), (2, 1)], [(0, 2)], [(0, 3)]],
            [[(1, 0)], [(1, 1)], [(1, 2), (3, 0)], [(1, 3), (3, 1)]],
        ],
    )
    for mine_b, mine_a in ((p_b2, p_a2), (p_b1, p_a1)):
        down, up = shift(to_b, "z", 8, -1), shift(to_a, "z", 8, 1)
        to_b, to_a = merge([mine_b, mine_a, down, up], [both(0, 2), both(1, 3)])
    down, up = shift(to_b, "z", 8, -1), shift(to_a, "z", 8, 1)
    (mine,) = merge([p_own, down, up], [[[(0, g), (1, g), (2, g)] for g in range(4)]])
    parts = [mine[:1]] + [shift(mine[step : step + 1], "y", 4, -step) for step in (1, 2, 3)]
    (attn,) = merge(parts, [[[(i, 0) for i in range(4)]]], final=True)

    keep, give = project(here, gather_z(gather_y(attn)), out_weight)
    sums = keep + shift(give, "core", 2, 1)
    low = sums.astype(BF16)
    total = sums[0]
    for step in (1, 2, 3):
        total = total + shift(low[step], "x", 4, step).astype(F32)
    return total.reshape(128, out_weight.shape[1]).astype(BF16)


def solution(mesh):
    split = Mesh(mesh.devices.reshape(4, 2, 4, 8), ("x", "core", "y", "z"))
    heads, store = ("x", "core"), ("y", "z")
    return jax.shard_map(
        per_device,
        mesh=split,
        in_specs=(
            P(store, heads, None, None),
            P(store, heads, None, None),
            P(store, heads, None, None),
            P(store, None),
            P(store),
            P(heads, store),
        ),
        out_specs=P(heads, store),
        check_vma=False,
    )
```

```python
import functools
import math

import jax
import jax.numpy as jnp
from jax import lax
from jax.experimental import pallas as pl
from jax.experimental.pallas import tpu as pltpu
from jax.sharding import Mesh, PartitionSpec as P

HEADS = 8
HEAD = 128
FLAT = HEADS * HEAD
WIDE = FLAT + 128
NEG = -1e30
BIG = 1e30
EXP_SCALE = HEAD**-0.5 * math.log2(math.e)
F32 = jnp.float32
BF16 = jnp.bfloat16
SUM_SENT = BF16
VMEM_LIMIT = 28 * 1024 * 1024


def shift(x, axis, size, step):
    return lax.ppermute(x, axis, [(i, (i + step) % size) for i in range(size)])


def lane_ids(rows):
    return lax.broadcasted_iota(jnp.int32, (rows, 128), 1)


def pack_stats(stats):
    lane = lane_ids(stats.shape[0])
    spread = jnp.where(
        (lane // 8) % 3 == 0,
        stats,
        jnp.where((lane // 8) % 3 == 1, pltpu.roll(stats, 8, 1), pltpu.roll(stats, 16, 1)),
    )
    high = spread.astype(BF16).astype(F32)
    rest = spread - high
    middle = rest.astype(BF16).astype(F32)
    low = rest - middle
    terms = jnp.where(
        (lane // 8) % 3 == 0, high, jnp.where((lane // 8) % 3 == 1, middle, low)
    )
    return jnp.where(lane < 48, terms, 0.0).astype(BF16)


def unpack_stats(packed):
    terms = packed.astype(F32)
    return terms + (pltpu.roll(terms, 120, 1) + pltpu.roll(terms, 112, 1))


def find_spans(me, q):
    code = q[:, FLAT:].astype(F32)
    span = jnp.where(code > 0, code - 1.0, 255.0 - code) - 16.0 * me
    mine = (code != 0) & (span >= 0) & (span < 16)
    first = jnp.min(jnp.where(mine, span, 99.0))
    second = jnp.max(jnp.where(mine, span, -1.0))
    picks = []
    for chosen in (first, second):
        live = jnp.max(jnp.where(mine & (span == chosen), 1.0, 0.0), axis=1, keepdims=True)
        at = jnp.clip(chosen.astype(jnp.int32), 0, 15)
        picks.append((at, jnp.concatenate([live] * HEADS, axis=0) > 0))
    return picks


def score(q, picks, k_ref):
    queries = jnp.concatenate([q[:, h * HEAD : (h + 1) * HEAD] for h in range(HEADS)], axis=0)
    return [
        lax.dot_general(queries, k_ref[at], (((1,), (1,)), ((), ())), preferred_element_type=F32)
        for at, _ in picks
    ]


def weigh(scores, picks, v_ref):
    top = None
    for s, (_, live) in zip(scores, picks):
        lanes = [s[:, i : i + 128] for i in range(0, s.shape[1], 128)]
        part = jnp.where(live, functools.reduce(jnp.maximum, lanes), NEG)
        top = part if top is None else jnp.maximum(top, part)
    top = jnp.max(top, axis=1, keepdims=True)
    both = None
    for s, (at, live) in zip(scores, picks):
        probs = jnp.exp2((s - jnp.where(live, top, BIG)) * EXP_SCALE).astype(BF16)
        span = v_ref[at]
        ones = jnp.concatenate([span, jnp.ones_like(span)], axis=1)
        out = jnp.dot(probs, ones, preferred_element_type=F32)
        both = out if both is None else both + out
    rows = top.shape[0] // HEADS
    lane = lane_ids(rows)
    stats = jnp.zeros((rows, 128), F32)
    heads = []
    for h in range(HEADS):
        part = slice(h * rows, (h + 1) * rows)
        denom = both[part, HEAD : HEAD + 1]
        stats = jnp.where(lane == h, top[part], jnp.where(lane == 24 + h, denom, stats))
        heads.append(both[part, :HEAD])
    return heads, stats


def put_packed(out_ref, at, heads, stats):
    for h, numer in enumerate(heads):
        out_ref[at, :, h * HEAD : (h + 1) * HEAD] = numer.astype(BF16)
    out_ref[at, :, FLAT:] = pack_stats(stats)


def attend_kernel(layout, before, me_ref, *refs):
    count = 1 + max(ref for ref, _, _, _ in layout)
    q_refs, (k_ref, v_ref), refs = refs[:count], refs[count : count + 2], refs[count + 2 :]
    outs = refs[-4:]
    for out, done in zip(outs, refs[:-4]):
        out[:before] = done[...]
    me = me_ref[0].astype(F32)
    picks = [find_spans(me, q_refs[ref][at]) for ref, at, _, _ in layout]
    ahead = score(q_refs[layout[0][0]][layout[0][1]], picks[0], k_ref)
    for i, (_, _, b, g) in enumerate(layout):
        scores = ahead
        if i + 1 < len(layout):
            ref, at, _, _ = layout[i + 1]
            ahead = score(q_refs[ref][at], picks[i + 1], k_ref)
        heads, stats = weigh(scores, picks[i], v_ref)
        if g:
            put_packed(outs[g], before + b, heads, stats)
            continue
        for h, numer in enumerate(heads):
            outs[0][before + b, :, h * HEAD : (h + 1) * HEAD] = numer
        outs[0][before + b, :, FLAT:] = stats


def local_call(kernel, name, scalars, inputs, out_shape, flops=0, exps=0):
    vmem = pl.BlockSpec(memory_space=pltpu.VMEM)
    size = sum(i.size * i.dtype.itemsize for i in list(inputs) + list(out_shape))
    return pl.pallas_call(
        kernel,
        out_shape=out_shape,
        in_specs=[pl.BlockSpec(memory_space=pltpu.SMEM)] * len(scalars) + [vmem] * len(inputs),
        out_specs=[vmem] * len(out_shape),
        compiler_params=pltpu.CompilerParams(vmem_limit_bytes=VMEM_LIMIT),
        cost_estimate=pl.CostEstimate(flops=flops, bytes_accessed=size, transcendentals=exps),
        name=name,
    )(*scalars, *inputs)


def attend(me, parts, keys, values, done=()):
    layout, place = [], 0
    for ref, part in enumerate(parts):
        for at in range(part.shape[0]):
            layout.append((ref, at, place // 4, place % 4))
            place += 1
    rows, before = parts[0].shape[1], done[0].shape[0] if done else 0
    out = [
        jax.ShapeDtypeStruct((before + place // 4, rows, WIDE), t) for t in (F32, BF16, BF16, BF16)
    ]
    work = place * 256 * 1024
    return local_call(
        functools.partial(attend_kernel, layout, before),
        "attend",
        [me],
        [*parts, keys, values, *done],
        out,
        flops=work * 4 * HEAD,
        exps=work,
    )


def packed_part(ref, at):
    return ref[at, :, :FLAT], unpack_stats(ref[at, :, FLAT:])


def join(parts):
    top = functools.reduce(jnp.maximum, [s for _, s in parts])
    weights = [jnp.exp2((s - top) * EXP_SCALE) for _, s in parts]
    denom = functools.reduce(
        jnp.add, [pltpu.roll(w, 24, 1) * s for w, (_, s) in zip(weights, parts)]
    )
    heads = []
    for h in range(HEADS):
        lanes = slice(h * HEAD, (h + 1) * HEAD)
        heads.append(
            functools.reduce(
                jnp.add,
                [w[:, h : h + 1] * n[:, lanes].astype(F32) for w, (n, _) in zip(weights, parts)],
            )
        )
    return heads, top, denom


def line_kernel(batches, first, z_ref, *refs):
    out_ref, mine_ref = refs[-2:]
    z = z_ref[0]
    if first:
        out_ref[...], mine_ref[...] = refs[-4][...], refs[-3][...]
    place = first
    for batch, size in enumerate(batches):
        own_ref, got = refs[4 * batch], refs[4 * batch + 1 : 4 * batch + 4]
        for b in range(size):
            step, place = STEPS[place], place + 1
            parts = [(own_ref[b, :, :FLAT], own_ref[b, :, FLAT:])]
            heads, top, denom = join(parts + [packed_part(r, b) for r in got])
            stats = jnp.where(lane_ids(top.shape[0]) < 24, top, denom)
            put_packed(out_ref, lax.rem(z + step + 8, 8), heads, stats)
            if step == 0:
                for h, numer in enumerate(heads):
                    mine_ref[:, h * HEAD : (h + 1) * HEAD] = numer
                mine_ref[:, FLAT:] = stats


def finish_kernel(z_ref, mine_ref, got_ref, out_ref):
    z = z_ref[0]
    parts = [(mine_ref[:, :FLAT], mine_ref[:, FLAT:])]
    parts += [packed_part(got_ref, lax.rem(z + step, 8)) for step in range(1, 8)]
    heads, _, denom = join(parts)
    for h, numer in enumerate(heads):
        attn = (numer / denom[:, 24 + h : 25 + h]).astype(BF16)
        for copy in range(8):
            out_ref[copy, :, h * HEAD : (h + 1) * HEAD] = attn


def project_kernel(core_ref, turn_ref, attn_ref, *refs):
    w_refs, (keep_ref, give_ref) = refs[:4], refs[4:]
    core = core_ref[0]
    for out_ref, half in ((give_ref, 1 - core), (keep_ref, core)):
        rows = attn_ref[pl.ds(half * 4, 4)].reshape(-1, FLAT)
        for back, w_ref in enumerate(w_refs):
            out_ref[lax.rem(turn_ref[0] - back + 8, 4)] = jnp.dot(
                rows, w_ref[...], preferred_element_type=F32
            )


STEPS = (0, -1, 1, -2, 2, -3, 3, 4)


def per_device(query_heads, span_keys, span_values, cited_spans, cite_count, out_weight):
    rows, columns = query_heads.shape[0], out_weight.shape[1]
    x, core, y, z = (lax.axis_index(a).astype(jnp.int32) for a in ("x", "core", "y", "z"))
    me, my_z = (y * 8 + z).reshape(1), z.reshape(1)
    slot = jnp.arange(cited_spans.shape[1], dtype=jnp.int32)
    code = jnp.where(cited_spans < 256, cited_spans + 1, 255 - cited_spans)
    code = jnp.where(slot[None, :] < cite_count[:, None], code, 0).astype(BF16)
    wide = jnp.concatenate(
        [query_heads.reshape(rows, FLAT), code, jnp.zeros((rows, 128 - code.shape[1]), BF16)], axis=1
    )
    keys, values = span_keys[:, 0], span_values[:, 0]

    def send(parts):
        return [parts[0]] + [shift(o, "y", 4, -s) for s, o in zip((1, 2, 3), parts[1:])]

    tie = lax.optimization_barrier
    own = jnp.stack([wide] + [shift(wide, "y", 4, step) for step in (1, 2, 3)])
    low_1, high_1 = shift(own, "z", 8, 1), shift(own, "z", 8, -1)
    near = attend(me, [own], keys, values)
    low_1, high_1, near = tie((low_1, high_1, near))
    low_2, high_2 = shift(low_1, "z", 8, 1), shift(high_1, "z", 8, -1)
    near = attend(me, [low_1, high_1], keys, values, near)
    weights = [shift(out_weight, "y", 4, step) for step in (1, 3)]
    low_2, high_2, near = tie((low_2, high_2, near))
    low_3, high_3 = shift(low_2, "z", 8, 1), shift(high_2, "z", 8, -1)
    near = attend(me, [low_2, high_2], keys, values, near)
    low_3, high_3, near, weights, out_weight = tie((low_3, high_3, near, weights, out_weight))
    far = [shift(low_3[:2], "z", 8, 1), shift(high_3[2:], "z", 8, -1)]
    near = send(near)
    beyond = attend(me, [low_3, high_3], keys, values)
    far, beyond, out_weight = tie((far, beyond, out_weight))
    beyond = send(attend(me, far, keys, values, beyond))
    weights = [out_weight, weights[0], shift(out_weight, "y", 4, 2), weights[1]]

    line = [jax.ShapeDtypeStruct((8, rows, WIDE), BF16), jax.ShapeDtypeStruct((rows, WIDE), F32)]
    joined = local_call(functools.partial(line_kernel, [5], 0), "line", [my_z], near, line)
    joined, mine = local_call(
        functools.partial(line_kernel, [3], 5), "line", [my_z], [*beyond, *joined], line
    )
    got = lax.all_to_all(joined, "z", 0, 0, tiled=True)
    got, weights = tie((got, weights))
    (attn,) = local_call(
        finish_kernel, "finish", [my_z], [mine, got], [jax.ShapeDtypeStruct((8, rows, FLAT), BF16)]
    )
    attn = lax.all_to_all(attn, "z", 0, 0, tiled=True)

    half = jax.ShapeDtypeStruct((4, 4 * rows, columns), F32)
    keep, give = local_call(
        project_kernel,
        "project",
        [core.reshape(1), (y - x).reshape(1)],
        [attn, *weights],
        [half, half],
        flops=2 * 1024 * FLAT * columns,
    )
    sums = keep + shift(give, "core", 2, 1)
    total = sums[0]
    for step in (1, 2, 3):
        total = total + shift(sums[step].astype(SUM_SENT), "x", 4, step).astype(F32)
    swap = [(a * 4 + b, b * 4 + a) for a in range(4) for b in range(4)]
    return lax.ppermute(total.astype(BF16), ("x", "y"), swap)


def solution(mesh):
    split = Mesh(mesh.devices.reshape(4, 2, 4, 8), ("x", "core", "y", "z"))
    heads, store = ("x", "core"), ("y", "z")
    return jax.shard_map(
        per_device,
        mesh=split,
        in_specs=(
            P(store, heads, None, None),
            P(store, heads, None, None),
            P(store, heads, None, None),
            P(store, None),
            P(store),
            P(heads, store),
        ),
        out_specs=P(heads, store),
        check_vma=False,
    )
```

```python
import functools
import math

import jax
import jax.numpy as jnp
from jax import lax
from jax.experimental import pallas as pl
from jax.experimental.pallas import tpu as pltpu
from jax.sharding import Mesh, PartitionSpec as P

HEADS = 8
HEAD = 128
FLAT = HEADS * HEAD
WIDE = FLAT + 128
NEG = -1e30
BIG = 1e30
EXP_SCALE = HEAD**-0.5 * math.log2(math.e)
F32 = jnp.float32
BF16 = jnp.bfloat16
VMEM_LIMIT = 28 * 1024 * 1024


def shift(x, axis, size, step):
    return lax.ppermute(x, axis, [(i, (i + step) % size) for i in range(size)])


def lane_ids(rows):
    return lax.broadcasted_iota(jnp.int32, (rows, 128), 1)


def pack_stats(stats):
    lane = lane_ids(stats.shape[0])
    spread = jnp.where(
        (lane // 8) % 3 == 0,
        stats,
        jnp.where((lane // 8) % 3 == 1, pltpu.roll(stats, 8, 1), pltpu.roll(stats, 16, 1)),
    )
    high = spread.astype(BF16).astype(F32)
    rest = spread - high
    middle = rest.astype(BF16).astype(F32)
    low = rest - middle
    terms = jnp.where(
        (lane // 8) % 3 == 0, high, jnp.where((lane // 8) % 3 == 1, middle, low)
    )
    return jnp.where(lane < 48, terms, 0.0).astype(BF16)


def unpack_stats(packed):
    terms = packed.astype(F32)
    return terms + (pltpu.roll(terms, 120, 1) + pltpu.roll(terms, 112, 1))


def find_spans(me, q):
    code = q[:, FLAT:].astype(F32)
    span = jnp.where(code > 0, code - 1.0, 255.0 - code) - 16.0 * me
    mine = (code != 0) & (span >= 0) & (span < 16)
    first = jnp.min(jnp.where(mine, span, 99.0))
    second = jnp.max(jnp.where(mine, span, -1.0))
    picks = []
    for chosen in (first, second):
        live = jnp.max(jnp.where(mine & (span == chosen), 1.0, 0.0), axis=1, keepdims=True)
        at = jnp.clip(chosen.astype(jnp.int32), 0, 15)
        picks.append((at, jnp.concatenate([live] * HEADS, axis=0) > 0))
    return picks


def score(q, picks, k_ref):
    queries = jnp.concatenate([q[:, h * HEAD : (h + 1) * HEAD] for h in range(HEADS)], axis=0)
    return [
        lax.dot_general(queries, k_ref[at], (((1,), (1,)), ((), ())), preferred_element_type=F32)
        for at, _ in picks
    ]


def weigh(scores, picks, v_ref):
    top = None
    for s, (_, live) in zip(scores, picks):
        lanes = [s[:, i : i + 128] for i in range(0, s.shape[1], 128)]
        part = jnp.where(live, functools.reduce(jnp.maximum, lanes), NEG)
        top = part if top is None else jnp.maximum(top, part)
    top = jnp.max(top, axis=1, keepdims=True)
    both = None
    for s, (at, live) in zip(scores, picks):
        probs = jnp.exp2((s - jnp.where(live, top, BIG)) * EXP_SCALE).astype(BF16)
        span = v_ref[at]
        ones = jnp.concatenate([span, jnp.ones_like(span)], axis=1)
        out = jnp.dot(probs, ones, preferred_element_type=F32)
        both = out if both is None else both + out
    rows = top.shape[0] // HEADS
    lane = lane_ids(rows)
    stats = jnp.zeros((rows, 128), F32)
    heads = []
    for h in range(HEADS):
        part = slice(h * rows, (h + 1) * rows)
        denom = both[part, HEAD : HEAD + 1]
        stats = jnp.where(lane == h, top[part], jnp.where(lane == 24 + h, denom, stats))
        heads.append(both[part, :HEAD])
    return heads, stats


def put_packed(out_ref, at, heads, stats):
    for h, numer in enumerate(heads):
        out_ref[at, :, h * HEAD : (h + 1) * HEAD] = numer.astype(BF16)
    out_ref[at, :, FLAT:] = pack_stats(stats)


def attend_kernel(layout, before, me_ref, *refs):
    count = 1 + max(ref for ref, _, _, _ in layout)
    q_refs, (k_ref, v_ref), refs = refs[:count], refs[count : count + 2], refs[count + 2 :]
    outs = refs[-4:]
    for out, done in zip(outs, refs[:-4]):
        out[:before] = done[...]
    me = me_ref[0].astype(F32)
    picks = [find_spans(me, q_refs[ref][at]) for ref, at, _, _ in layout]
    ahead = score(q_refs[layout[0][0]][layout[0][1]], picks[0], k_ref)
    for i, (_, _, b, g) in enumerate(layout):
        scores = ahead
        if i + 1 < len(layout):
            ref, at, _, _ = layout[i + 1]
            ahead = score(q_refs[ref][at], picks[i + 1], k_ref)
        heads, stats = weigh(scores, picks[i], v_ref)
        if g:
            put_packed(outs[g], before + b, heads, stats)
            continue
        for h, numer in enumerate(heads):
            outs[0][before + b, :, h * HEAD : (h + 1) * HEAD] = numer
        outs[0][before + b, :, FLAT:] = stats


def local_call(kernel, name, scalars, inputs, out_shape, flops=0, exps=0):
    vmem = pl.BlockSpec(memory_space=pltpu.VMEM)
    size = sum(i.size * i.dtype.itemsize for i in list(inputs) + list(out_shape))
    return pl.pallas_call(
        kernel,
        out_shape=out_shape,
        in_specs=[pl.BlockSpec(memory_space=pltpu.SMEM)] * len(scalars) + [vmem] * len(inputs),
        out_specs=[vmem] * len(out_shape),
        compiler_params=pltpu.CompilerParams(vmem_limit_bytes=VMEM_LIMIT),
        cost_estimate=pl.CostEstimate(flops=flops, bytes_accessed=size, transcendentals=exps),
        name=name,
    )(*scalars, *inputs)


def attend(me, parts, keys, values, done=()):
    layout, place = [], 0
    for ref, part in enumerate(parts):
        for at in range(part.shape[0]):
            layout.append((ref, at, place // 4, place % 4))
            place += 1
    rows, before = parts[0].shape[1], done[0].shape[0] if done else 0
    out = [
        jax.ShapeDtypeStruct((before + place // 4, rows, WIDE), t) for t in (F32, BF16, BF16, BF16)
    ]
    work = place * 256 * 1024
    return local_call(
        functools.partial(attend_kernel, layout, before),
        "attend",
        [me],
        [*parts, keys, values, *done],
        out,
        flops=work * 4 * HEAD,
        exps=work,
    )


def packed_part(ref, at):
    return ref[at, :, :FLAT], unpack_stats(ref[at, :, FLAT:])


def join(parts):
    top = functools.reduce(jnp.maximum, [s for _, s in parts])
    weights = [jnp.exp2((s - top) * EXP_SCALE) for _, s in parts]
    denom = functools.reduce(
        jnp.add, [pltpu.roll(w, 24, 1) * s for w, (_, s) in zip(weights, parts)]
    )
    heads = []
    for h in range(HEADS):
        lanes = slice(h * HEAD, (h + 1) * HEAD)
        heads.append(
            functools.reduce(
                jnp.add,
                [w[:, h : h + 1] * n[:, lanes].astype(F32) for w, (n, _) in zip(weights, parts)],
            )
        )
    return heads, top, denom


def line_kernel(batches, first, z_ref, *refs):
    out_ref, mine_ref = refs[-2:]
    z = z_ref[0]
    if first:
        out_ref[...], mine_ref[...] = refs[-4][...], refs[-3][...]
    place = first
    for batch, size in enumerate(batches):
        own_ref, got = refs[4 * batch], refs[4 * batch + 1 : 4 * batch + 4]
        for b in range(size):
            step, place = STEPS[place], place + 1
            parts = [(own_ref[b, :, :FLAT], own_ref[b, :, FLAT:])]
            heads, top, denom = join(parts + [packed_part(r, b) for r in got])
            stats = jnp.where(lane_ids(top.shape[0]) < 24, top, denom)
            put_packed(out_ref, lax.rem(z + step + 8, 8), heads, stats)
            if step == 0:
                for h, numer in enumerate(heads):
                    mine_ref[:, h * HEAD : (h + 1) * HEAD] = numer
                mine_ref[:, FLAT:] = stats


def finish_kernel(z_ref, mine_ref, got_ref, out_ref):
    z = z_ref[0]
    parts = [(mine_ref[:, :FLAT], mine_ref[:, FLAT:])]
    parts += [packed_part(got_ref, lax.rem(z + step, 8)) for step in range(1, 8)]
    heads, _, denom = join(parts)
    for h, numer in enumerate(heads):
        attn = (numer / denom[:, 24 + h : 25 + h]).astype(BF16)
        for copy in range(8):
            out_ref[copy, :, h * HEAD : (h + 1) * HEAD] = attn


SUM_AT = (0, 2, 1, 3)


def project_kernel(core_ref, turn_ref, attn_ref, *refs):
    w_refs, (keep_ref, give_ref) = refs[:4], refs[4:]
    core = core_ref[0]
    for out_ref, half in ((give_ref, 1 - core), (keep_ref, core)):
        rows = attn_ref[pl.ds(half * 4, 4)].reshape(-1, FLAT)
        for back, w_ref in enumerate(w_refs):
            out_ref[lax.rem(turn_ref[0] + SUM_AT[back] + 4, 4)] = jnp.dot(
                rows, w_ref[...], preferred_element_type=F32
            )


STEPS = (0, -1, 1, -2, 2, -3, 3, 4)


def per_device(query_heads, span_keys, span_values, cited_spans, cite_count, out_weight):
    rows, columns = query_heads.shape[0], out_weight.shape[1]
    x, core, y, z = (lax.axis_index(a).astype(jnp.int32) for a in ("x", "core", "y", "z"))
    me, my_z = (y * 8 + z).reshape(1), z.reshape(1)
    slot = jnp.arange(cited_spans.shape[1], dtype=jnp.int32)
    code = jnp.where(cited_spans < 256, cited_spans + 1, 255 - cited_spans)
    code = jnp.where(slot[None, :] < cite_count[:, None], code, 0).astype(BF16)
    wide = jnp.concatenate(
        [query_heads.reshape(rows, FLAT), code, jnp.zeros((rows, 128 - code.shape[1]), BF16)], axis=1
    )
    keys, values = span_keys[:, 0], span_values[:, 0]

    def send(parts):
        return [parts[0]] + [shift(o, "y", 4, -s) for s, o in zip((1, 2, 3), parts[1:])]

    tie = lax.optimization_barrier
    own = jnp.stack([wide] + [shift(wide, "y", 4, step) for step in (1, 2, 3)])
    low_1, high_1 = shift(own, "z", 8, 1), shift(own, "z", 8, -1)
    near = attend(me, [own], keys, values)
    low_1, high_1, near = tie((low_1, high_1, near))
    low_2, high_2 = shift(low_1, "z", 8, 1), shift(high_1, "z", 8, -1)
    near = attend(me, [low_1, high_1], keys, values, near)
    weights = [shift(out_weight, "y", 4, step) for step in (1, 3)]
    low_2, high_2, near = tie((low_2, high_2, near))
    low_3, high_3 = shift(low_2, "z", 8, 1), shift(high_2, "z", 8, -1)
    near = send(near)
    second = attend(me, [low_2, high_2], keys, values)
    low_3, high_3, second, weights, out_weight = tie((low_3, high_3, second, weights, out_weight))
    far = shift(low_3, "z", 8, 1)
    second = send(second)
    low_3, high_3, near = tie((low_3, high_3, near))
    third = attend(me, [low_3, high_3], keys, values)
    far, third, second, out_weight = tie((far, third, second, out_weight))
    third = send(attend(me, [far], keys, values, third))
    weights = [out_weight, weights[0], shift(out_weight, "y", 4, 2), weights[1]]

    line = [jax.ShapeDtypeStruct((8, rows, WIDE), BF16), jax.ShapeDtypeStruct((rows, WIDE), F32)]
    joined = local_call(
        functools.partial(line_kernel, [3, 2], 0), "line", [my_z], [*near, *second], line
    )
    joined, mine = local_call(
        functools.partial(line_kernel, [3], 5), "line", [my_z], [*third, *joined], line
    )
    got = lax.all_to_all(joined, "z", 0, 0, tiled=True)
    got, weights = tie((got, weights))
    (attn,) = local_call(
        finish_kernel, "finish", [my_z], [mine, got], [jax.ShapeDtypeStruct((8, rows, FLAT), BF16)]
    )
    attn = lax.all_to_all(attn, "z", 0, 0, tiled=True)

    half = jax.ShapeDtypeStruct((4, 4 * rows, columns), F32)
    keep, give = local_call(
        project_kernel,
        "project",
        [core.reshape(1), (y - x).reshape(1)],
        [attn, *weights],
        [half, half],
        flops=2 * 1024 * FLAT * columns,
    )
    sums = keep + shift(give, "core", 2, 1)
    total = sums[0]
    for step in (1, 2, 3):
        total = total + shift(sums[step].astype(BF16), "x", 4, step).astype(F32)
    swap = [
        ((b + at) % 4 * 4 + b, b * 4 + (b - back) % 4) for b in range(4) for back, at in enumerate(SUM_AT)
    ]
    return lax.ppermute(total.astype(BF16), ("x", "y"), swap)


def solution(mesh):
    split = Mesh(mesh.devices.reshape(4, 2, 4, 8), ("x", "core", "y", "z"))
    heads, store = ("x", "core"), ("y", "z")
    return jax.shard_map(
        per_device,
        mesh=split,
        in_specs=(
            P(store, heads, None, None),
            P(store, heads, None, None),
            P(store, heads, None, None),
            P(store, None),
            P(store),
            P(heads, store),
        ),
        out_specs=P(heads, store),
        check_vma=False,
    )
```

```python
import functools
import math

import jax
import jax.numpy as jnp
from jax import lax
from jax.experimental import pallas as pl
from jax.experimental.pallas import tpu as pltpu
from jax.sharding import Mesh, PartitionSpec as P

HEADS = 8
HEAD = 128
FLAT = HEADS * HEAD
WIDE = FLAT + 128
NEG = -1e30
BIG = 1e30
EXP_SCALE = HEAD**-0.5 * math.log2(math.e)
F32 = jnp.float32
BF16 = jnp.bfloat16
VMEM_LIMIT = 28 * 1024 * 1024


def shift(x, axis, size, step):
    return lax.ppermute(x, axis, [(i, (i + step) % size) for i in range(size)])


def lane_ids(rows):
    return lax.broadcasted_iota(jnp.int32, (rows, 128), 1)


def pack_stats(stats):
    lane = lane_ids(stats.shape[0])
    spread = jnp.where(
        (lane // 8) % 3 == 0,
        stats,
        jnp.where((lane // 8) % 3 == 1, pltpu.roll(stats, 8, 1), pltpu.roll(stats, 16, 1)),
    )
    high = spread.astype(BF16).astype(F32)
    rest = spread - high
    middle = rest.astype(BF16).astype(F32)
    low = rest - middle
    terms = jnp.where(
        (lane // 8) % 3 == 0, high, jnp.where((lane // 8) % 3 == 1, middle, low)
    )
    return jnp.where(lane < 48, terms, 0.0).astype(BF16)


def unpack_stats(packed):
    terms = packed.astype(F32)
    return terms + (pltpu.roll(terms, 120, 1) + pltpu.roll(terms, 112, 1))


def find_spans(me, q):
    code = q[:, FLAT:].astype(F32)
    span = jnp.where(code > 0, code - 1.0, 255.0 - code) - 16.0 * me
    mine = (code != 0) & (span >= 0) & (span < 16)
    first = jnp.min(jnp.where(mine, span, 99.0))
    second = jnp.max(jnp.where(mine, span, -1.0))
    picks = []
    for chosen in (first, second):
        live = jnp.max(jnp.where(mine & (span == chosen), 1.0, 0.0), axis=1, keepdims=True)
        at = jnp.clip(chosen.astype(jnp.int32), 0, 15)
        picks.append((at, jnp.concatenate([live] * HEADS, axis=0) > 0))
    return picks


def score(q, picks, k_ref):
    queries = jnp.concatenate([q[:, h * HEAD : (h + 1) * HEAD] for h in range(HEADS)], axis=0)
    return [
        lax.dot_general(queries, k_ref[at], (((1,), (1,)), ((), ())), preferred_element_type=F32)
        for at, _ in picks
    ]


def weigh(scores, picks, v_ref):
    top = None
    for s, (_, live) in zip(scores, picks):
        lanes = [s[:, i : i + 128] for i in range(0, s.shape[1], 128)]
        part = jnp.where(live, functools.reduce(jnp.maximum, lanes), NEG)
        top = part if top is None else jnp.maximum(top, part)
    top = jnp.max(top, axis=1, keepdims=True)
    both = None
    for s, (at, live) in zip(scores, picks):
        probs = jnp.exp2((s - jnp.where(live, top, BIG)) * EXP_SCALE).astype(BF16)
        span = v_ref[at]
        ones = jnp.concatenate([span, jnp.ones_like(span)], axis=1)
        out = jnp.dot(probs, ones, preferred_element_type=F32)
        both = out if both is None else both + out
    rows = top.shape[0] // HEADS
    lane = lane_ids(rows)
    stats = jnp.zeros((rows, 128), F32)
    heads = []
    for h in range(HEADS):
        part = slice(h * rows, (h + 1) * rows)
        denom = both[part, HEAD : HEAD + 1]
        stats = jnp.where(lane == h, top[part], jnp.where(lane == 24 + h, denom, stats))
        heads.append(both[part, :HEAD])
    return heads, stats


def put_packed(out_ref, at, heads, stats):
    for h, numer in enumerate(heads):
        out_ref[at, :, h * HEAD : (h + 1) * HEAD] = numer.astype(BF16)
    out_ref[at, :, FLAT:] = pack_stats(stats)


def attend_kernel(layout, before, me_ref, *refs):
    count = 1 + max(ref for ref, _, _, _ in layout)
    q_refs, (k_ref, v_ref), refs = refs[:count], refs[count : count + 2], refs[count + 2 :]
    outs = refs[-4:]
    for out, done in zip(outs, refs[:-4]):
        out[:before] = done[...]
    me = me_ref[0].astype(F32)
    picks = [find_spans(me, q_refs[ref][at]) for ref, at, _, _ in layout]
    ahead = score(q_refs[layout[0][0]][layout[0][1]], picks[0], k_ref)
    for i, (_, _, b, g) in enumerate(layout):
        scores = ahead
        if i + 1 < len(layout):
            ref, at, _, _ = layout[i + 1]
            ahead = score(q_refs[ref][at], picks[i + 1], k_ref)
        heads, stats = weigh(scores, picks[i], v_ref)
        if g:
            put_packed(outs[g], before + b, heads, stats)
            continue
        for h, numer in enumerate(heads):
            outs[0][before + b, :, h * HEAD : (h + 1) * HEAD] = numer
        outs[0][before + b, :, FLAT:] = stats


def local_call(kernel, name, scalars, inputs, out_shape, flops=0, exps=0):
    vmem = pl.BlockSpec(memory_space=pltpu.VMEM)
    size = sum(i.size * i.dtype.itemsize for i in list(inputs) + list(out_shape))
    return pl.pallas_call(
        kernel,
        out_shape=out_shape,
        in_specs=[pl.BlockSpec(memory_space=pltpu.SMEM)] * len(scalars) + [vmem] * len(inputs),
        out_specs=[vmem] * len(out_shape),
        compiler_params=pltpu.CompilerParams(vmem_limit_bytes=VMEM_LIMIT),
        cost_estimate=pl.CostEstimate(flops=flops, bytes_accessed=size, transcendentals=exps),
        name=name,
    )(*scalars, *inputs)


def attend(me, parts, keys, values, done=()):
    layout, place = [], 0
    for ref, part in enumerate(parts):
        for at in range(part.shape[0]):
            layout.append((ref, at, place // 4, place % 4))
            place += 1
    rows, before = parts[0].shape[1], done[0].shape[0] if done else 0
    out = [
        jax.ShapeDtypeStruct((before + place // 4, rows, WIDE), t) for t in (F32, BF16, BF16, BF16)
    ]
    work = place * 256 * 1024
    return local_call(
        functools.partial(attend_kernel, layout, before),
        "attend",
        [me],
        [*parts, keys, values, *done],
        out,
        flops=work * 4 * HEAD,
        exps=work,
    )


def packed_part(ref, at):
    return ref[at, :, :FLAT], unpack_stats(ref[at, :, FLAT:])


def join(parts):
    top = functools.reduce(jnp.maximum, [s for _, s in parts])
    weights = [jnp.exp2((s - top) * EXP_SCALE) for _, s in parts]
    denom = functools.reduce(
        jnp.add, [pltpu.roll(w, 24, 1) * s for w, (_, s) in zip(weights, parts)]
    )
    heads = []
    for h in range(HEADS):
        lanes = slice(h * HEAD, (h + 1) * HEAD)
        heads.append(
            functools.reduce(
                jnp.add,
                [w[:, h : h + 1] * n[:, lanes].astype(F32) for w, (n, _) in zip(weights, parts)],
            )
        )
    return heads, top, denom


def line_kernel(batches, first, z_ref, *refs):
    out_ref, mine_ref = refs[-2:]
    z = z_ref[0]
    if first:
        out_ref[...], mine_ref[...] = refs[-4][...], refs[-3][...]
    place = first
    for batch, size in enumerate(batches):
        own_ref, got = refs[4 * batch], refs[4 * batch + 1 : 4 * batch + 4]
        for b in range(size):
            step, place = STEPS[place], place + 1
            parts = [(own_ref[b, :, :FLAT], own_ref[b, :, FLAT:])]
            heads, top, denom = join(parts + [packed_part(r, b) for r in got])
            stats = jnp.where(lane_ids(top.shape[0]) < 24, top, denom)
            put_packed(out_ref, lax.rem(z + step + 8, 8), heads, stats)
            if step == 0:
                for h, numer in enumerate(heads):
                    mine_ref[:, h * HEAD : (h + 1) * HEAD] = numer
                mine_ref[:, FLAT:] = stats


def finish_kernel(z_ref, mine_ref, got_ref, out_ref):
    z = z_ref[0]
    parts = [(mine_ref[:, :FLAT], mine_ref[:, FLAT:])]
    parts += [packed_part(got_ref, lax.rem(z + step, 8)) for step in range(1, 8)]
    heads, _, denom = join(parts)
    for h, numer in enumerate(heads):
        attn = (numer / denom[:, 24 + h : 25 + h]).astype(BF16)
        for copy in range(8):
            out_ref[copy, :, h * HEAD : (h + 1) * HEAD] = attn


SUM_AT = (2, 3, 0, 1)


def project_kernel(core_ref, turn_ref, attn_ref, *refs):
    w_refs, (keep_ref, give_ref) = refs[:4], refs[4:]
    core = core_ref[0]
    for out_ref, half in ((give_ref, 1 - core), (keep_ref, core)):
        rows = attn_ref[pl.ds(half * 4, 4)].reshape(-1, FLAT)
        for back, w_ref in enumerate(w_refs):
            out_ref[lax.rem(turn_ref[0] + SUM_AT[back] + 4, 4)] = jnp.dot(
                rows, w_ref[...], preferred_element_type=F32
            )


STEPS = (0, -1, 1, -2, 2, -3, 3, 4)


def per_device(query_heads, span_keys, span_values, cited_spans, cite_count, out_weight):
    rows, columns = query_heads.shape[0], out_weight.shape[1]
    x, core, y, z = (lax.axis_index(a).astype(jnp.int32) for a in ("x", "core", "y", "z"))
    me, my_z = (y * 8 + z).reshape(1), z.reshape(1)
    slot = jnp.arange(cited_spans.shape[1], dtype=jnp.int32)
    code = jnp.where(cited_spans < 256, cited_spans + 1, 255 - cited_spans)
    code = jnp.where(slot[None, :] < cite_count[:, None], code, 0).astype(BF16)
    wide = jnp.concatenate(
        [query_heads.reshape(rows, FLAT), code, jnp.zeros((rows, 128 - code.shape[1]), BF16)], axis=1
    )
    keys, values = span_keys[:, 0], span_values[:, 0]

    def send(parts):
        return [parts[0]] + [shift(o, "y", 4, -s) for s, o in zip((1, 2, 3), parts[1:])]

    tie = lax.optimization_barrier
    own = jnp.stack([wide] + [shift(wide, "y", 4, step) for step in (1, 2, 3)])
    low_1, high_1 = shift(own, "z", 8, 1), shift(own, "z", 8, -1)
    near = attend(me, [own], keys, values)
    low_1, high_1, near = tie((low_1, high_1, near))
    low_2, high_2 = shift(low_1, "z", 8, 1), shift(high_1, "z", 8, -1)
    near = attend(me, [low_1, high_1], keys, values, near)
    low_2, high_2, near = tie((low_2, high_2, near))
    low_3, high_3 = shift(low_2, "z", 8, 1), shift(high_2, "z", 8, -1)
    near = send(near)
    second = attend(me, [low_2, high_2], keys, values)
    low_3, high_3, second = tie((low_3, high_3, second))
    far = shift(low_3, "z", 8, 1)
    second = send(second)
    low_3, high_3, near = tie((low_3, high_3, near))
    third = attend(me, [low_3, high_3], keys, values)
    far, third, second, out_weight = tie((far, third, second, out_weight))
    third = send(attend(me, [far], keys, values, third))
    across = shift(out_weight, "y", 4, 2)

    line = [jax.ShapeDtypeStruct((8, rows, WIDE), BF16), jax.ShapeDtypeStruct((rows, WIDE), F32)]
    joined = local_call(
        functools.partial(line_kernel, [3, 2], 0), "line", [my_z], [*near, *second], line
    )
    joined, mine = local_call(
        functools.partial(line_kernel, [3], 5), "line", [my_z], [*third, *joined], line
    )
    got = lax.all_to_all(joined, "z", 0, 0, tiled=True)
    got, across = tie((got, across))
    (attn,) = local_call(
        finish_kernel, "finish", [my_z], [mine, got], [jax.ShapeDtypeStruct((8, rows, FLAT), BF16)]
    )
    attn, out_weight = tie((attn, out_weight))
    attn = lax.all_to_all(attn, "z", 0, 0, tiled=True)
    weights = [out_weight, shift(out_weight, "y", 4, 1), across, shift(out_weight, "y", 4, 3)]

    half = jax.ShapeDtypeStruct((4, 4 * rows, columns), F32)
    keep, give = local_call(
        project_kernel,
        "project",
        [core.reshape(1), (y - x).reshape(1)],
        [attn, *weights],
        [half, half],
        flops=2 * 1024 * FLAT * columns,
    )
    sums = keep + shift(give, "core", 2, 1)
    total = sums[0]
    for step in (1, 2, 3):
        total = total + shift(sums[step].astype(BF16), "x", 4, step).astype(F32)
    swap = [
        ((b + at) % 4 * 4 + b, b * 4 + (b - back) % 4) for b in range(4) for back, at in enumerate(SUM_AT)
    ]
    return lax.ppermute(total.astype(BF16), ("x", "y"), swap)


def solution(mesh):
    split = Mesh(mesh.devices.reshape(4, 2, 4, 8), ("x", "core", "y", "z"))
    heads, store = ("x", "core"), ("y", "z")
    return jax.shard_map(
        per_device,
        mesh=split,
        in_specs=(
            P(store, heads, None, None),
            P(store, heads, None, None),
            P(store, heads, None, None),
            P(store, None),
            P(store),
            P(heads, store),
        ),
        out_specs=P(heads, store),
        check_vma=False,
    )
```

```python
import functools
import math

import jax
import jax.numpy as jnp
from jax import lax
from jax.experimental import pallas as pl
from jax.experimental.pallas import tpu as pltpu
from jax.sharding import Mesh, PartitionSpec as P

HEADS = 8
HEAD = 128
FLAT = HEADS * HEAD
WIDE = FLAT + 128
NEG = -1e30
BIG = 1e30
EXP_SCALE = HEAD**-0.5 * math.log2(math.e)
F32 = jnp.float32
BF16 = jnp.bfloat16
VMEM_LIMIT = 28 * 1024 * 1024


def shift(x, axis, size, step):
    return lax.ppermute(x, axis, [(i, (i + step) % size) for i in range(size)])


def lane_ids(rows):
    return lax.broadcasted_iota(jnp.int32, (rows, 128), 1)


def pack_stats(stats):
    lane = lane_ids(stats.shape[0])
    spread = jnp.where(
        (lane // 8) % 3 == 0,
        stats,
        jnp.where((lane // 8) % 3 == 1, pltpu.roll(stats, 8, 1), pltpu.roll(stats, 16, 1)),
    )
    high = spread.astype(BF16).astype(F32)
    rest = spread - high
    middle = rest.astype(BF16).astype(F32)
    low = rest - middle
    terms = jnp.where(
        (lane // 8) % 3 == 0, high, jnp.where((lane // 8) % 3 == 1, middle, low)
    )
    return jnp.where(lane < 48, terms, 0.0).astype(BF16)


def unpack_stats(packed):
    terms = packed.astype(F32)
    return terms + (pltpu.roll(terms, 120, 1) + pltpu.roll(terms, 112, 1))


def find_spans(me, q):
    code = q[:, FLAT:].astype(F32)
    span = jnp.where(code > 0, code - 1.0, 255.0 - code) - 16.0 * me
    mine = (code != 0) & (span >= 0) & (span < 16)
    first = jnp.min(jnp.where(mine, span, 99.0))
    second = jnp.max(jnp.where(mine, span, -1.0))
    picks = []
    for chosen in (first, second):
        live = jnp.max(jnp.where(mine & (span == chosen), 1.0, 0.0), axis=1, keepdims=True)
        at = jnp.clip(chosen.astype(jnp.int32), 0, 15)
        picks.append((at, jnp.concatenate([live] * HEADS, axis=0) > 0))
    return picks


def score(q, picks, k_ref):
    queries = jnp.concatenate([q[:, h * HEAD : (h + 1) * HEAD] for h in range(HEADS)], axis=0)
    return [
        lax.dot_general(queries, k_ref[at], (((1,), (1,)), ((), ())), preferred_element_type=F32)
        for at, _ in picks
    ]


def weigh(scores, picks, v_ref):
    top = None
    for s, (_, live) in zip(scores, picks):
        lanes = [s[:, i : i + 128] for i in range(0, s.shape[1], 128)]
        part = jnp.where(live, functools.reduce(jnp.maximum, lanes), NEG)
        top = part if top is None else jnp.maximum(top, part)
    top = jnp.max(top, axis=1, keepdims=True)
    both = None
    for s, (at, live) in zip(scores, picks):
        probs = jnp.exp2((s - jnp.where(live, top, BIG)) * EXP_SCALE).astype(BF16)
        span = v_ref[at]
        ones = jnp.concatenate([span, jnp.ones_like(span)], axis=1)
        out = jnp.dot(probs, ones, preferred_element_type=F32)
        both = out if both is None else both + out
    rows = top.shape[0] // HEADS
    lane = lane_ids(rows)
    stats = jnp.zeros((rows, 128), F32)
    heads = []
    for h in range(HEADS):
        part = slice(h * rows, (h + 1) * rows)
        denom = both[part, HEAD : HEAD + 1]
        stats = jnp.where(lane == h, top[part], jnp.where(lane == 24 + h, denom, stats))
        heads.append(both[part, :HEAD])
    return heads, stats


def put_packed(out_ref, at, heads, stats):
    for h, numer in enumerate(heads):
        out_ref[at, :, h * HEAD : (h + 1) * HEAD] = numer.astype(BF16)
    out_ref[at, :, FLAT:] = pack_stats(stats)


def attend_kernel(layout, before, me_ref, *refs):
    count = 1 + max(ref for ref, _, _, _ in layout)
    q_refs, (k_ref, v_ref), refs = refs[:count], refs[count : count + 2], refs[count + 2 :]
    outs = refs[-4:]
    for out, done in zip(outs, refs[:-4]):
        out[:before] = done[...]
    me = me_ref[0].astype(F32)
    picks = [find_spans(me, q_refs[ref][at]) for ref, at, _, _ in layout]
    ahead = score(q_refs[layout[0][0]][layout[0][1]], picks[0], k_ref)
    for i, (_, _, b, g) in enumerate(layout):
        scores = ahead
        if i + 1 < len(layout):
            ref, at, _, _ = layout[i + 1]
            ahead = score(q_refs[ref][at], picks[i + 1], k_ref)
        heads, stats = weigh(scores, picks[i], v_ref)
        if g:
            put_packed(outs[g], before + b, heads, stats)
            continue
        for h, numer in enumerate(heads):
            outs[0][before + b, :, h * HEAD : (h + 1) * HEAD] = numer
        outs[0][before + b, :, FLAT:] = stats


def local_call(kernel, name, scalars, inputs, out_shape, flops=0, exps=0):
    vmem = pl.BlockSpec(memory_space=pltpu.VMEM)
    size = sum(i.size * i.dtype.itemsize for i in list(inputs) + list(out_shape))
    return pl.pallas_call(
        kernel,
        out_shape=out_shape,
        in_specs=[pl.BlockSpec(memory_space=pltpu.SMEM)] * len(scalars) + [vmem] * len(inputs),
        out_specs=[vmem] * len(out_shape),
        compiler_params=pltpu.CompilerParams(vmem_limit_bytes=VMEM_LIMIT),
        cost_estimate=pl.CostEstimate(flops=flops, bytes_accessed=size, transcendentals=exps),
        name=name,
    )(*scalars, *inputs)


def attend(me, parts, keys, values, done=()):
    layout, place = [], 0
    for ref, part in enumerate(parts):
        for at in range(part.shape[0]):
            layout.append((ref, at, place // 4, place % 4))
            place += 1
    rows, before = parts[0].shape[1], done[0].shape[0] if done else 0
    out = [
        jax.ShapeDtypeStruct((before + place // 4, rows, WIDE), t) for t in (F32, BF16, BF16, BF16)
    ]
    work = place * 256 * 1024
    return local_call(
        functools.partial(attend_kernel, layout, before),
        "attend",
        [me],
        [*parts, keys, values, *done],
        out,
        flops=work * 4 * HEAD,
        exps=work,
    )


def packed_part(ref, at):
    return ref[at, :, :FLAT], unpack_stats(ref[at, :, FLAT:])


def join(parts):
    top = functools.reduce(jnp.maximum, [s for _, s in parts])
    weights = [jnp.exp2((s - top) * EXP_SCALE) for _, s in parts]
    denom = functools.reduce(
        jnp.add, [pltpu.roll(w, 24, 1) * s for w, (_, s) in zip(weights, parts)]
    )
    heads = []
    for h in range(HEADS):
        lanes = slice(h * HEAD, (h + 1) * HEAD)
        heads.append(
            functools.reduce(
                jnp.add,
                [w[:, h : h + 1] * n[:, lanes].astype(F32) for w, (n, _) in zip(weights, parts)],
            )
        )
    return heads, top, denom


def line_kernel(batches, first, z_ref, *refs):
    out_ref, mine_ref = refs[-2:]
    z = z_ref[0]
    if first:
        out_ref[...], mine_ref[...] = refs[-4][...], refs[-3][...]
    place = first
    for batch, size in enumerate(batches):
        own_ref, got = refs[4 * batch], refs[4 * batch + 1 : 4 * batch + 4]
        for b in range(size):
            step, place = STEPS[place], place + 1
            parts = [(own_ref[b, :, :FLAT], own_ref[b, :, FLAT:])]
            heads, top, denom = join(parts + [packed_part(r, b) for r in got])
            stats = jnp.where(lane_ids(top.shape[0]) < 24, top, denom)
            put_packed(out_ref, lax.rem(z + step + 8, 8), heads, stats)
            if step == 0:
                for h, numer in enumerate(heads):
                    mine_ref[:, h * HEAD : (h + 1) * HEAD] = numer
                mine_ref[:, FLAT:] = stats


def finish_kernel(z_ref, mine_ref, got_ref, out_ref):
    z = z_ref[0]
    parts = [(mine_ref[:, :FLAT], mine_ref[:, FLAT:])]
    parts += [packed_part(got_ref, lax.rem(z + step, 8)) for step in range(1, 8)]
    heads, _, denom = join(parts)
    for h, numer in enumerate(heads):
        attn = (numer / denom[:, 24 + h : 25 + h]).astype(BF16)
        for copy in range(8):
            out_ref[copy, :, h * HEAD : (h + 1) * HEAD] = attn


SUM_AT = (2, 3, 0, 1)


def project_kernel(core_ref, turn_ref, attn_ref, *refs):
    w_refs, (keep_ref, give_ref) = refs[:4], refs[4:]
    core = core_ref[0]
    for out_ref, half in ((give_ref, 1 - core), (keep_ref, core)):
        rows = attn_ref[pl.ds(half * 4, 4)].reshape(-1, FLAT)
        for back, w_ref in enumerate(w_refs):
            out_ref[lax.rem(turn_ref[0] + SUM_AT[back] + 4, 4)] = jnp.dot(
                rows, w_ref[...], preferred_element_type=F32
            )


STEPS = (0, -1, 1, -2, 2, -3, 3, 4)


def per_device(query_heads, span_keys, span_values, cited_spans, cite_count, out_weight):
    rows, columns = query_heads.shape[0], out_weight.shape[1]
    x, core, y, z = (lax.axis_index(a).astype(jnp.int32) for a in ("x", "core", "y", "z"))
    me, my_z = (y * 8 + z).reshape(1), z.reshape(1)
    slot = jnp.arange(cited_spans.shape[1], dtype=jnp.int32)
    code = jnp.where(cited_spans < 256, cited_spans + 1, 255 - cited_spans)
    code = jnp.where(slot[None, :] < cite_count[:, None], code, 0).astype(BF16)
    wide = jnp.concatenate(
        [query_heads.reshape(rows, FLAT), code, jnp.zeros((rows, 128 - code.shape[1]), BF16)], axis=1
    )
    keys, values = span_keys[:, 0], span_values[:, 0]

    def send(parts):
        return [parts[0]] + [shift(o, "y", 4, -s) for s, o in zip((1, 2, 3), parts[1:])]

    tie = lax.optimization_barrier
    own = jnp.stack([wide] + [shift(wide, "y", 4, step) for step in (1, 2, 3)])
    low_1, high_1 = shift(own, "z", 8, 1), shift(own, "z", 8, -1)
    near = attend(me, [own], keys, values)
    low_1, high_1, near = tie((low_1, high_1, near))
    low_2, high_2 = shift(low_1, "z", 8, 1), shift(high_1, "z", 8, -1)
    near = attend(me, [low_1, high_1], keys, values, near)
    across = shift(out_weight, "y", 4, 2)
    low_2, high_2, near = tie((low_2, high_2, near))
    low_3, high_3 = shift(low_2, "z", 8, 1), shift(high_2, "z", 8, -1)
    near = send(near)
    second = attend(me, [low_2, high_2], keys, values)
    low_3, high_3, second, across, out_weight = tie((low_3, high_3, second, across, out_weight))
    far = shift(low_3, "z", 8, 1)
    second = send(second)
    low_3, high_3, near = tie((low_3, high_3, near))
    third = attend(me, [low_3, high_3], keys, values)
    far, third, second, out_weight = tie((far, third, second, out_weight))
    third = send(attend(me, [far], keys, values, third))
    beside = [shift(out_weight, "y", 4, step) for step in (1, 3)]

    line = [jax.ShapeDtypeStruct((8, rows, WIDE), BF16), jax.ShapeDtypeStruct((rows, WIDE), F32)]
    joined = local_call(
        functools.partial(line_kernel, [3, 2], 0), "line", [my_z], [*near, *second], line
    )
    joined, mine = local_call(
        functools.partial(line_kernel, [3], 5), "line", [my_z], [*third, *joined], line
    )
    got = lax.all_to_all(joined, "z", 0, 0, tiled=True)
    (attn,) = local_call(
        finish_kernel, "finish", [my_z], [mine, got], [jax.ShapeDtypeStruct((8, rows, FLAT), BF16)]
    )
    attn, beside = tie((attn, beside))
    attn = lax.all_to_all(attn, "z", 0, 0, tiled=True)
    weights = [out_weight, beside[0], across, beside[1]]

    half = jax.ShapeDtypeStruct((4, 4 * rows, columns), F32)
    keep, give = local_call(
        project_kernel,
        "project",
        [core.reshape(1), (y - x).reshape(1)],
        [attn, *weights],
        [half, half],
        flops=2 * 1024 * FLAT * columns,
    )
    sums = keep + shift(give, "core", 2, 1)
    total = sums[0]
    for step in (1, 2, 3):
        total = total + shift(sums[step].astype(BF16), "x", 4, step).astype(F32)
    swap = [
        ((b + at) % 4 * 4 + b, b * 4 + (b - back) % 4) for b in range(4) for back, at in enumerate(SUM_AT)
    ]
    return lax.ppermute(total.astype(BF16), ("x", "y"), swap)


def solution(mesh):
    split = Mesh(mesh.devices.reshape(4, 2, 4, 8), ("x", "core", "y", "z"))
    heads, store = ("x", "core"), ("y", "z")
    return jax.shard_map(
        per_device,
        mesh=split,
        in_specs=(
            P(store, heads, None, None),
            P(store, heads, None, None),
            P(store, heads, None, None),
            P(store, None),
            P(store),
            P(heads, store),
        ),
        out_specs=P(heads, store),
        check_vma=False,
    )
```
